256 devices in a mesh: mem: 8 (over x, core), expert: 32 (over z, y).
Axes of the slice: x: 4, y: 4, z: 8, core: 2. Of those that a mesh axis runs over, the one named last changes fastest.
Arguments:
- queries: bfloat16 [65536, 4096], P(('mem', 'expert')), may hold values from -128 to 128
- out_grad: bfloat16 [65536, 4096], P(('mem', 'expert')), may hold values from -12 to 12
- mem_keys: bfloat16 [8192, 4096], P('mem', 'expert'), may hold values from -4.5 to 4.5
- mem_values: bfloat16 [8192, 4096], P('mem', 'expert'), may hold values from -48 to 48
- block_index: int32 [512, 4], P('mem'), may hold values from 0 to 63, as said below
- routes: int32 [65536, 2], P(('mem', 'expert')), may hold values from 0 to 31, all different within a row; in each aligned block of 256 rows (0 to 255, 256 to 511, ...) at most 24 rows name the same one
- combine: bfloat16 [65536, 2], P(('mem', 'expert')), may hold values from 0.049804688 to 1
- gate_pre: bfloat16 [32, 6144, 768], P('expert', 'mem'), may hold values from -6 to 6
- up_pre: bfloat16 [32, 6144, 768], P('expert', 'mem'), may hold values from -6 to 6
- w_down: bfloat16 [32, 768, 4096], P('expert', 'mem'), may hold values from -0.21875 to 0.21875
Outputs:
- query_grad: bfloat16 [65536, 4096], P('mem', 'expert')
- w_down_grad: bfloat16 [32, 768, 4096], P('expert', 'mem')
- gate_grad: bfloat16 [32, 6144, 768], P('expert', 'mem')
- up_grad: bfloat16 [32, 6144, 768], P('expert', 'mem')
- combine_grad: float32 [32, 6144], P('expert', 'mem')
The draws below stay inside these ranges and needn't reach their ends.
Inputs may be any that keep to these rules, and one draw needn't show every extreme that they name: `block_index`: each row names 4 memory blocks of 4 different owner groups, where block c belongs to group c // 8. `routes`: each row names 2 different experts; within the 256 rows of one device no expert is named by more than 24 rows, a bound that some block reaches.
All inputs are finite; a program needn't handle non-finite values.
Results may differ from the reference program's by a relative error of at most 0.013.
Values may be sent and summed in bfloat16 or wider, within the bound.
No kernel may reach another device: no remote copies, remote signals or barrier semaphores. Data moves between devices by JAX's collectives and lax.ppermute only.
A program may use at most 192 MiB of HBM per device.

```python
import math
import jax
import jax.numpy as jnp
import numpy as np
from jax import lax

HEADS = 32
HD = 128
D = 4096
FF = 768
EXPERTS = 32
TOPK = 2
QBLK = 128
KSEL = 4
TOK_DEV = 256
MB_DEV = 8
TOKENS = 65536
NQB = 512
NMB = 64
CAP = 24
SLOTS = 6144
N_MEM = 8
N_EXPERT = 32


def draw_block_index(key, part):
    base_key = jax.random.fold_in(key, 11)
    row_keys = jax.random.split(base_key, NQB)
    owner_ids = jax.vmap(lambda row_key: jax.random.permutation(row_key, N_MEM)[:KSEL])(row_keys)
    within = jax.random.randint(jax.random.fold_in(key, 14), (NQB, KSEL), 0, MB_DEV)
    return (owner_ids * MB_DEV + within).astype(jnp.int32)


def key_rows(key):
    base_draw = jax.random.truncated_normal(jax.random.fold_in(key, 12), -4.5, 4.5, (NMB, QBLK, D), jnp.float32)
    return base_draw


def draw_mem_keys(key, part):
    return key_rows(key).reshape(NMB * QBLK, D).astype(jnp.bfloat16)


def draw_queries(key, part):
    drawn_draw = jax.random.truncated_normal(jax.random.fold_in(key, 13), -4.5, 4.5, (NQB, QBLK, D), jnp.float32)
    return drawn_draw.reshape(TOKENS, D).astype(jnp.bfloat16)


def steps_of(stream_key, extent, cuts, smallest, high):
    factor_of, own = 1.0, jax.random.fold_in(stream_key, 6)
    for axis_at, blocks in cuts:
        steps = jnp.exp(jax.random.uniform(jax.random.fold_in(own, axis_at), (blocks,), jnp.float32, smallest / len(cuts), high / len(cuts)))
        factor_of = factor_of * jnp.repeat(steps, extent[axis_at] // blocks).reshape([-1 if axis == axis_at else 1 for axis in range(len(extent))])
    return factor_of


def routed_block(stream_key, own, number, rows, number_of, top, most, lean):
    order = jax.random.permutation(stream_key, number_of)
    heavy_load, common = load_shares(number_of, rows * top, most, lean, True), load_shares(number_of, rows * top, most, lean, False)
    places = jnp.arange(number_of)

    def named(sizes, rotation):
        used = int((sizes > 0).sum())
        fixed = max(1, used // 4)
        passed = fixed + (places - fixed + rotation * (used - fixed)) % max(1, number_of - fixed)
        return jnp.zeros((number_of,), jnp.int32).at[order[jnp.where(places < fixed, places, passed)]].set(jnp.asarray(sizes, jnp.int32))

    sizes = jnp.where(number % 4 == 0, named(heavy_load, number // 4), named(common, number - number // 4 - 1))
    mixed = jax.random.permutation(jax.random.fold_in(own, 3), number_of)
    source_of, receiver = mixed[0:number_of // 2 * 2:2], mixed[1:number_of // 2 * 2:2]
    slack = jnp.minimum(sizes[source_of] - 1, most - sizes[receiver]) // 2
    slack = jnp.where((source_of == order[0]) | (receiver == order[0]) | (sizes[receiver] == 0), 0, jnp.maximum(slack, 0))
    passed = jax.random.randint(jax.random.fold_in(own, 4), (number_of // 2,), 0, 1 << 20) % (slack + 1)
    sizes = sizes.at[source_of].add(-passed).at[receiver].add(passed)
    members = jnp.searchsorted(jnp.cumsum(sizes), jnp.arange(rows * top), side="right").astype(jnp.int32)
    listing = members.reshape(top, rows).T
    listing = listing[jax.random.permutation(jax.random.fold_in(own, 1), rows)]
    rotation = jax.random.randint(jax.random.fold_in(own, 2), (rows, 1), 0, top)
    return jnp.take_along_axis(listing, (jnp.arange(top)[None, :] + rotation) % top, axis=1)


def load_shares(amount, total, most, lean, full):
    weights = [(1 << 20) // math.isqrt(rank ** lean) + 1 for rank in range(1, amount + 1)]
    largest = most if full else min(most, max(-(-total // amount), total * weights[0] // sum(weights)))
    least = 1 if total - largest >= amount - 1 else 0
    counts, rest = [largest] + [least] * (amount - 1), total - largest - least * (amount - 1)
    while rest > 0:
        movable = [i for i in range(1, amount) if counts[i] < largest] or [i for i in range(1, amount) if counts[i] < most]
        whole, remaining = sum([weights[i] for i in movable]), rest
        for i in movable:
            extra = min(most - counts[i], max(1, remaining * weights[i] // whole), rest)
            counts[i] = counts[i] + extra
            rest = rest - extra
    return np.array(counts)


def scatter_about(stream_key, shape, width, reach, cuts=(), held_as=jnp.bfloat16):
    values = jax.random.normal(stream_key, shape, jnp.float32) * width
    if len(cuts) > 0:
        values = steps_of(stream_key, shape, cuts, -0.22, 0.18) * values
    return jnp.clip(values, min=-reach, max=reach).astype(held_as)


def setup_inputs(seed: int = 0) -> dict:
    streams_of = jax.random.split(jax.random.key(seed), 11)
    queries = draw_queries(jax.random.fold_in(streams_of[10], 71), 0)
    out_grad = scatter_about(streams_of[1], (TOKENS, D), 2.0, 12.0, ((0, 256),))
    mem_keys = draw_mem_keys(jax.random.fold_in(streams_of[10], 71), 0)
    mem_values = scatter_about(streams_of[3], (NMB * QBLK, D), 8.0, 48.0, ((0, 8), (1, 32)))
    block_index = draw_block_index(jax.random.fold_in(streams_of[10], 71), 0)
    routes_keys = jax.random.split(jax.random.fold_in(streams_of[5], 1), TOKENS // TOK_DEV)
    routes_turns = jax.random.permutation(jax.random.fold_in(streams_of[5], 3), TOKENS // TOK_DEV)
    routes = jax.vmap(lambda own, number: routed_block(jax.random.fold_in(streams_of[5], 2), own, number, TOK_DEV, EXPERTS, TOPK, CAP, 2))(routes_keys, routes_turns).reshape((TOKENS, TOPK))
    combine = jnp.clip(jnp.exp(math.log(1.0) - 2.9996462 * jax.random.uniform(streams_of[6], (TOKENS, TOPK), jnp.float32) ** steps_of(streams_of[6], (TOKENS, TOPK), ((0, 256),), -0.2, 0.2)), 0.049804688, 1.0).astype(jnp.bfloat16)
    gate_pre = scatter_about(streams_of[7], (EXPERTS, SLOTS, FF), 1.0, 6.0, ((0, 32), (1, 8)))
    up_pre = scatter_about(streams_of[8], (EXPERTS, SLOTS, FF), 1.0, 6.0, ((0, 32), (1, 8)))
    w_down = scatter_about(streams_of[9], (EXPERTS, FF, D), FF ** -0.5, 0.21875, ((0, 32), (1, 8)))
    return {"queries": queries, "out_grad": out_grad, "mem_keys": mem_keys, "mem_values": mem_values, "block_index": block_index, "routes": routes, "combine": combine, "gate_pre": gate_pre, "up_pre": up_pre, "w_down": w_down}


def attend_block(inputs, keys_table, values_table):
    query_rows, grad_rows, chosen = inputs
    score_scale = 1.0 / (HD ** 0.5)
    picked_keys = keys_table[chosen].reshape(KSEL * QBLK, HEADS, HD).astype(jnp.float32)
    picked_values = values_table[chosen].reshape(KSEL * QBLK, HEADS, HD).astype(jnp.float32)
    scores = jnp.einsum("qhd,khd->hqk", query_rows.astype(jnp.float32), picked_keys) * score_scale
    highest = jnp.max(scores, axis=-1, keepdims=True)
    weights = jnp.exp(scores - highest)
    probabilities = weights / jnp.sum(weights, axis=-1, keepdims=True)
    grad_probs = jnp.einsum("qhd,khd->hqk", grad_rows.astype(jnp.float32), picked_values)
    delta_sum = jnp.sum(probabilities * grad_probs, axis=-1, keepdims=True)
    grad_scores = (probabilities * (grad_probs - delta_sum)).astype(jnp.bfloat16)
    result = jnp.einsum("hqk,khd->qhd", grad_scores.astype(jnp.float32), picked_keys) * score_scale
    return result.astype(jnp.bfloat16)


def expert_grads(inputs, out_grad):
    slot_token, slot_weight, gate_slots, up_slots, weight_rows = inputs
    present = slot_token >= 0
    slot_rows = jnp.where(present[:, None], out_grad[jnp.maximum(slot_token, 0)], jnp.zeros((), jnp.bfloat16))
    back_grad = jnp.dot(slot_rows, weight_rows.T, preferred_element_type=jnp.float32)
    gate_val = gate_slots.astype(jnp.float32)
    up_val = up_slots.astype(jnp.float32)
    sigmoid_gate = jax.nn.sigmoid(gate_val)
    silu_gate = gate_val * sigmoid_gate
    hidden = silu_gate * up_val
    combine_grad = jnp.sum(hidden * back_grad, axis=-1)
    hidden_grad = slot_weight[:, None] * back_grad
    gate_grad = (hidden_grad * up_val * sigmoid_gate * (1.0 + gate_val * (1.0 - sigmoid_gate))).astype(jnp.bfloat16)
    up_grad = (hidden_grad * silu_gate).astype(jnp.bfloat16)
    weighted = (slot_weight[:, None] * hidden).astype(jnp.bfloat16)
    group_rows = SLOTS // N_MEM
    group_terms = jnp.einsum("gsf,gsd->gfd", weighted.reshape(N_MEM, group_rows, FF).astype(jnp.float32), slot_rows.reshape(N_MEM, group_rows, D).astype(jnp.float32))
    rounded_terms = lax.optimization_barrier(group_terms.astype(jnp.bfloat16))
    down_grad = jnp.sum(rounded_terms.astype(jnp.float32), axis=0).astype(jnp.bfloat16)
    return down_grad, gate_grad, up_grad, combine_grad


def reference(queries, out_grad, mem_keys, mem_values, block_index, routes, combine, gate_pre, up_pre, w_down):
    keys_table = mem_keys.reshape(NMB, QBLK, HEADS, HD)
    values_table = mem_values.reshape(NMB, QBLK, HEADS, HD)
    query_grad = lax.map(lambda entries: attend_block(entries, keys_table, values_table), (queries.reshape(NQB, QBLK, HEADS, HD), out_grad.reshape(NQB, QBLK, HEADS, HD), block_index)).reshape(TOKENS, D)
    device_count = N_MEM * N_EXPERT
    source = routes.reshape(device_count, TOK_DEV, TOPK)
    named_count = jnp.sum((source[..., None] == jnp.arange(EXPERTS, dtype=jnp.int32)).astype(jnp.int32), axis=2, dtype=jnp.int32)
    before = jnp.cumsum(named_count, axis=1, dtype=jnp.int32) - named_count
    slot_rank = jnp.take_along_axis(before, source, axis=2).astype(jnp.int32)
    slot_index = (jnp.arange(device_count, dtype=jnp.int32)[:, None, None] * CAP + slot_rank).reshape(-1).astype(jnp.int32)
    expert_index = routes.reshape(-1).astype(jnp.int32)
    token_index = jnp.repeat(jnp.arange(TOKENS, dtype=jnp.int32), TOPK)
    slot_token = jnp.full((EXPERTS, SLOTS), -1, jnp.int32).at[expert_index, slot_index].set(token_index)
    slot_weight = jnp.zeros((EXPERTS, SLOTS), jnp.float32).at[expert_index, slot_index].set(combine.reshape(-1).astype(jnp.float32))
    down_grad, gate_grad, up_grad, combine_grad = lax.map(lambda entries: expert_grads(entries, out_grad), (slot_token, slot_weight, gate_pre, up_pre, w_down))
    return query_grad, down_grad, gate_grad, up_grad, combine_grad
```

```python
import functools

import jax
import jax.numpy as jnp
from jax import lax
from jax.experimental import pallas as pl
from jax.experimental.pallas import tpu as pltpu
from jax.sharding import PartitionSpec as P

HD = 128
QBLK = 128
YS = 4
NEAR = (0, -1, 1)
MID = (-2, 2)
FAR = (-3, 3)
OPPOSITE = (4,)
BANDS = 11


def move(x, zs, dz, dy):
    pairs = [
        (z * YS + y, ((z + dz) % zs) * YS + (y + dy) % YS) for z in range(zs) for y in range(YS)
    ]
    return lax.ppermute(x, "expert", pairs)


def move_opposite(x, zs, mems):
    experts = zs * YS
    pairs = []
    for m in range(mems):
        dz = 2 if m % 2 == 0 else -2
        for z in range(zs):
            for y in range(YS):
                pairs.append((m * experts + z * YS + y, m * experts + ((z + dz) % zs) * YS + y))
    return lax.ppermute(x, ("mem", "expert"), pairs)


def in_bands(block, cap):
    rows = block.astype(jnp.float32)
    fill = BANDS * cap - rows.shape[0]
    rows = jnp.concatenate([rows, jnp.zeros((fill, HD), jnp.float32)], axis=0)
    return [rows[t * cap : (t + 1) * cap].astype(jnp.bfloat16) for t in range(BANDS)]


def placing(ref, width, cap, plane, my_y, keep=None):
    table = ref[:, width:].astype(jnp.float32)
    toks = table.shape[0]
    r0, r1, c0, c1 = (table[:, i : i + 1] for i in range(4))
    lane = lax.broadcasted_iota(jnp.int32, (toks, HD), 1)
    step = sum((lane >= cap * i).astype(jnp.int32) for i in range(1, YS))
    rank = (lane - cap * step).astype(jnp.float32)
    turned = my_y + step
    turned = jnp.where(turned >= YS, turned - YS, turned)
    expert = jnp.where(lane < YS * cap, plane * YS + turned, -1).astype(jnp.float32)
    hit0, hit1 = r0 == expert, r1 == expert
    hit = jnp.where(hit0 | hit1, 1.0, 0.0)
    earlier = lax.broadcasted_iota(jnp.int32, (toks, toks), 1) < lax.broadcasted_iota(
        jnp.int32, (toks, toks), 0
    )
    before = jnp.dot(
        jnp.where(earlier, 1.0, 0.0).astype(jnp.bfloat16),
        hit.astype(jnp.bfloat16),
        preferred_element_type=jnp.float32,
    )
    placed = jnp.where(before == rank, hit, 0.0)
    if keep is not None:
        placed = jnp.where(keep, placed, 0.0)
    value = placed * (jnp.where(hit0, c0, 0.0) + jnp.where(hit1, c1, 0.0))
    weight = jnp.dot(
        value.T.astype(jnp.bfloat16),
        jnp.ones((toks, HD), jnp.bfloat16),
        preferred_element_type=jnp.float32,
    )
    return placed.T.astype(jnp.bfloat16), weight


def head_columns(ref, plane, my_y, j, cap):
    turned = lax.rem(my_y + j, YS)
    first = pl.multiple_of((plane * YS + turned) * HD, HD)
    return in_bands(ref[:, pl.ds(first, HD)], cap)


def dispatch_kernel(n_src, cap, width, info_ref, *refs):
    my_y, plane = info_ref[0], info_ref[1]
    outs = refs[n_src:]
    step = 1024
    for s in range(n_src):
        rows = refs[s]
        onehot, weight = placing(rows, width, cap, plane, my_y)
        for c in range(0, width, step):
            picked = jnp.dot(onehot, rows[:, c : c + step], preferred_element_type=jnp.float32)
            for j in range(YS):
                outs[j][s, :, c : c + step] = picked[j * cap : (j + 1) * cap].astype(jnp.bfloat16)
        for j in range(YS):
            outs[j][s, :, width : width + HD] = weight[j * cap : (j + 1) * cap].astype(
                jnp.bfloat16
            )
            for t, band in enumerate(head_columns(rows, plane, my_y, j, cap)):
                at = width + (1 + t) * HD
                outs[j][s, :, at : at + HD] = band


def dispatch(sources, info, cap):
    n_src = len(sources)
    toks, wide = sources[0].shape
    width = wide - HD
    out_shape = [jax.ShapeDtypeStruct((n_src, cap, wide + BANDS * HD), jnp.bfloat16)] * YS
    whole = pl.BlockSpec(memory_space=pltpu.VMEM)
    return pl.pallas_call(
        functools.partial(dispatch_kernel, n_src, cap, width),
        in_specs=[pl.BlockSpec(memory_space=pltpu.SMEM)] + [whole] * n_src,
        out_specs=[whole] * YS,
        out_shape=out_shape,
        compiler_params=pltpu.CompilerParams(vmem_limit_bytes=28 << 20),
        cost_estimate=pl.CostEstimate(
            flops=2 * n_src * 4 * cap * toks * width,
            bytes_accessed=2 * n_src * width * (toks + 4 * cap),
            transcendentals=0,
        ),
        name="dispatch",
    )(info, *sources)


def pack_kernel(cap, width, info_ref, low_ref, high_ref, *outs):
    my_y, core = info_ref[0], info_ref[1]
    above, below, far_up, far_down = (info_ref[2 + i] for i in range(4))
    step = 1024
    oh_above, w_above = placing(low_ref, width, cap, above, my_y)
    oh_below, w_below = placing(high_ref, width, cap, below, my_y)
    oh_up, w_up = placing(low_ref, width, cap, far_up, my_y, core == 0)
    oh_down, w_down = placing(high_ref, width, cap, far_down, my_y, core != 0)
    for c in range(0, width, step):
        low, high = low_ref[:, c : c + step], high_ref[:, c : c + step]
        picks = (
            jnp.dot(oh_above, low, preferred_element_type=jnp.float32),
            jnp.dot(oh_below, high, preferred_element_type=jnp.float32),
            jnp.dot(oh_up, low, preferred_element_type=jnp.float32)
            + jnp.dot(oh_down, high, preferred_element_type=jnp.float32),
        )
        for out, picked in zip(outs, picks):
            for j in range(YS):
                out[j, :, c : c + step] = picked[j * cap : (j + 1) * cap].astype(jnp.bfloat16)
    for out, w in zip(outs, (w_above, w_below, w_up + w_down)):
        for j in range(YS):
            out[j, :, width : width + HD] = w[j * cap : (j + 1) * cap].astype(jnp.bfloat16)

    def columns(out, ref, plane):
        for j in range(YS):
            for t, band in enumerate(head_columns(ref, plane, my_y, j, cap)):
                at = width + (1 + t) * HD
                out[j, :, at : at + HD] = band

    columns(outs[0], low_ref, above)
    columns(outs[1], high_ref, below)

    @pl.when(core == 0)
    def _():
        columns(outs[2], low_ref, far_up)

    @pl.when(core != 0)
    def _():
        columns(outs[2], high_ref, far_down)


def make_packs(low, high, info, cap):
    toks, wide = low.shape
    width = wide - HD
    whole = pl.BlockSpec(memory_space=pltpu.VMEM)
    return pl.pallas_call(
        functools.partial(pack_kernel, cap, width),
        in_specs=[pl.BlockSpec(memory_space=pltpu.SMEM)] + [whole] * 2,
        out_specs=[whole] * 3,
        out_shape=[jax.ShapeDtypeStruct((YS, cap, wide + BANDS * HD), jnp.bfloat16)] * 3,
        compiler_params=pltpu.CompilerParams(vmem_limit_bytes=28 << 20),
        cost_estimate=pl.CostEstimate(
            flops=2 * 4 * 4 * cap * toks * width,
            bytes_accessed=2 * 2 * width * (toks + 6 * cap),
            transcendentals=0,
        ),
        name="packs",
    )(info, low, high)


def restack_kernel(*refs):
    n = len(refs) - YS
    for j in range(YS):
        for p in range(n):
            refs[n + j][p] = refs[p][j]


def restack(packs):
    whole = pl.BlockSpec(memory_space=pltpu.VMEM)
    shape = (len(packs),) + packs[0].shape[1:]
    size = 2 * 2 * YS * shape[0] * shape[1] * shape[2]
    return pl.pallas_call(
        restack_kernel,
        in_specs=[whole] * len(packs),
        out_specs=[whole] * YS,
        out_shape=[jax.ShapeDtypeStruct(shape, packs[0].dtype)] * YS,
        compiler_params=pltpu.CompilerParams(vmem_limit_bytes=28 << 20),
        cost_estimate=pl.CostEstimate(flops=0, bytes_accessed=size, transcendentals=0),
        name="restack",
    )(*packs)


def attention_kernel(group, half, back_ref, chosen_ref, q_ref, *refs):
    g_refs = refs[:group]
    k_ref, v_ref = refs[group : group + 2]
    out_ref = refs[-1]
    scale = 1.0 / HD**0.5
    log2e = 1.4426950408889634
    contract_last = (((1,), (1,)), ((), ()))
    cap = g_refs[0].shape[1]
    first = half * QBLK // cap
    skip = half * QBLK - first * cap

    def start(i):
        block = (pl.program_id(0) * group + i) * 2 + half
        ids = [chosen_ref[block, c] for c in range(chosen_ref.shape[1])]
        keys = jnp.concatenate([k_ref[b] for b in ids], axis=0)
        values = jnp.concatenate([v_ref[b] for b in ids], axis=0)
        bands = [
            g_refs[i][0, :, t * HD : (t + 1) * HD].astype(jnp.float32)
            for t in range(first, first - (-(skip + QBLK) // cap))
        ]
        grads = jnp.concatenate(bands, axis=0)[skip : skip + QBLK].astype(jnp.bfloat16)
        scores = lax.dot_general(
            q_ref[i], keys, contract_last, preferred_element_type=jnp.float32
        )
        grad_probs = lax.dot_general(
            grads, values, contract_last, preferred_element_type=jnp.float32
        )
        return keys, scores, grad_probs

    def middle(keys, scores, grad_probs):
        highest = jnp.max(scores, axis=-1, keepdims=True)
        weights = jnp.exp2((scores - highest) * (scale * log2e))
        inverse = 1.0 / jnp.sum(weights, axis=-1, keepdims=True)
        delta = jnp.sum(weights * grad_probs, axis=-1, keepdims=True) * inverse
        return keys, (weights * (grad_probs - delta)).astype(jnp.bfloat16), inverse * scale

    def finish(i, keys, grad_scores, factor):
        total = jnp.dot(grad_scores, keys, preferred_element_type=jnp.float32)
        out_ref[i, 0] = (total * factor).astype(jnp.bfloat16)

    started, halfway = start(0), None
    for i in range(group):
        later = start(i + 1) if i + 1 < group else None
        now = middle(*started)
        if halfway is not None:
            finish(i - 1, *halfway)
        started, halfway = later, now
    finish(group - 1, *halfway)


def attention(half, back, chosen, q, g, keys, values, earlier):
    n_src = back.shape[0]
    group = 4
    full = lambda k, p, c: (0, 0, 0)
    in_specs = [pl.BlockSpec((group, QBLK, HD), lambda k, p, c: (k, 0, 0))]
    for i in range(group):
        in_specs.append(
            pl.BlockSpec((1,) + g.shape[1:], lambda k, p, c, i=i: (p[k * group + i], 0, 0))
        )
    in_specs += [pl.BlockSpec(keys.shape, full), pl.BlockSpec(values.shape, full)]
    args = [q] + [g] * group + [keys, values]
    aliases = {}
    if earlier is not None:
        in_specs.append(pl.BlockSpec(memory_space=pl.ANY))
        args.append(earlier)
        aliases = {2 + len(args) - 1: 0}
    return pl.pallas_call(
        functools.partial(attention_kernel, group, half),
        grid_spec=pltpu.PrefetchScalarGridSpec(
            num_scalar_prefetch=2,
            grid=(n_src // group,),
            in_specs=in_specs,
            out_specs=pl.BlockSpec((group, 1, QBLK, HD), lambda k, p, c: (k, half, 0, 0)),
        ),
        out_shape=jax.ShapeDtypeStruct((n_src, 2, QBLK, HD), jnp.bfloat16),
        input_output_aliases=aliases,
        compiler_params=pltpu.CompilerParams(vmem_limit_bytes=60 << 20),
        cost_estimate=pl.CostEstimate(
            flops=6 * n_src * QBLK * 512 * HD,
            bytes_accessed=6 * n_src * QBLK * HD + 4 * 64 * QBLK * HD,
            transcendentals=n_src * QBLK * 512,
        ),
        name="attention",
    )(back, chosen, *args)


def per_device(
    queries, out_grad, mem_keys, mem_values, block_index, routes, combine, gate_pre, up_pre, w_down
):
    experts = lax.axis_size("expert")
    mems = lax.axis_size("mem")
    zs = experts // YS
    me = lax.axis_index("expert")
    core = lax.axis_index("mem") % 2
    my_z, my_y = me // YS, me % YS
    toks, width = out_grad.shape
    cap = gate_pre.shape[1] // experts
    ff = gate_pre.shape[2]

    own = jnp.concatenate(
        [
            out_grad,
            routes.astype(jnp.bfloat16),
            combine,
            jnp.zeros((toks, HD - routes.shape[1] - combine.shape[1]), jnp.bfloat16),
        ],
        axis=1,
    )
    src = {0: own}
    src[-1] = move(own, zs, 1, 0)
    src[1] = move(own, zs, -1, 0)

    all_keys = lax.all_gather(mem_keys, "mem", axis=0, tiled=True)
    all_values = lax.all_gather(mem_values, "mem", axis=0, tiled=True)
    w_full = lax.all_gather(w_down, "mem", axis=1, tiled=True)[0]
    w_full = jnp.pad(w_full, ((0, 0), (0, HD)))

    place = jnp.stack(
        [
            ((my_z + dz) % zs) * YS + (my_y - j) % YS
            for stage in (NEAR, MID, FAR, OPPOSITE)
            for j in range(YS)
            for dz in stage
        ]
    ).astype(jnp.int32)
    back = jnp.zeros((experts,), jnp.int32).at[place].set(jnp.arange(experts, dtype=jnp.int32))

    gate_rel = jnp.take(gate_pre.reshape(experts, cap, ff), place, axis=0).reshape(-1, ff)
    up_rel = jnp.take(up_pre.reshape(experts, cap, ff), place, axis=0).reshape(-1, ff)
    gate_val = gate_rel.astype(jnp.float32)
    up_val = up_rel.astype(jnp.float32)
    sigmoid_gate = jax.nn.sigmoid(gate_val)
    silu_gate = gate_val * sigmoid_gate
    hidden = silu_gate * up_val

    src[-2] = move(src[-1], zs, 1, 0)
    src[2] = move(src[1], zs, -1, 0)
    here = jnp.stack([my_y, my_z]).astype(jnp.int32)

    def spread(x):
        return [x[0]] + [move(x[j], zs, 0, j) for j in range(1, YS)]

    near = spread(dispatch([src[dz] for dz in NEAR], here, cap))
    targets = [my_y, core] + [(my_z + dz) % zs for dz in (1, -1, 2, -2)]
    packs = make_packs(src[-2], src[2], jnp.stack(targets).astype(jnp.int32), cap)
    far = [move(packs[0], zs, 1, 0), move(packs[1], zs, -1, 0), move_opposite(packs[2], zs, mems)]
    low, high, packs, near = lax.optimization_barrier((src[-2], src[2], packs, near))
    mid = spread(dispatch([low, high], here, cap))

    by_half = [
        jnp.swapaxes(queries[h * QBLK : (h + 1) * QBLK].reshape(QBLK, experts, HD), 0, 1)
        for h in range(2)
    ]
    opposite = far.pop()
    by_half, far = lax.optimization_barrier((by_half, far))
    half_queries = [
        lax.all_to_all(by_half[0], "expert", split_axis=0, concat_axis=0, tiled=True)
    ]

    late = spread(restack(far)) + spread([opposite[j : j + 1] for j in range(YS)])
    early = near + mid
    n_early = YS * (len(NEAR) + len(MID)) * cap

    def slot_grads(pieces, span):
        rows = jnp.concatenate([a[:, :, : width + HD] for a in pieces], axis=0)
        rows = rows.reshape(-1, width + HD)
        weight_col = rows[:, width : width + 1].astype(jnp.float32)
        weighted = (weight_col * hidden[span]).astype(jnp.bfloat16)
        down = lax.dot_general(
            weighted, rows, (((0,), (0,)), ((), ())), preferred_element_type=jnp.float32
        )
        back_grad = lax.dot_general(
            rows, w_full, (((1,), (1,)), ((), ())), preferred_element_type=jnp.float32
        )
        gate, up, sig = gate_val[span], up_val[span], sigmoid_gate[span]
        hidden_grad = weight_col * back_grad
        return down, (
            (hidden_grad * up * sig * (1.0 + gate * (1.0 - sig))).astype(jnp.bfloat16),
            (hidden_grad * silu_gate[span]).astype(jnp.bfloat16),
            jnp.sum(hidden[span] * back_grad, axis=-1),
        )

    down_early, grads_early = slot_grads(early, slice(0, n_early))
    heads_early = jnp.concatenate([a[:, :, width + HD :] for a in early], axis=0)
    half_queries[0], late, by_half[1], down_early, grads_early, heads_early = (
        lax.optimization_barrier(
            (half_queries[0], late, by_half[1], down_early, grads_early, heads_early)
        )
    )
    half_queries.append(
        lax.all_to_all(by_half[1], "expert", split_axis=0, concat_axis=0, tiled=True)
    )
    down_late, grads_late = slot_grads(late, slice(n_early, None))
    down_total = down_early + down_late
    w_down_grad = lax.psum_scatter(
        down_total.astype(jnp.bfloat16), "mem", scatter_dimension=0, tiled=True
    )[None, :, :width]
    gate_grad, up_grad, combine_rel = (jnp.concatenate(r, axis=0) for r in zip(grads_early, grads_late))

    def restore(x):
        return jnp.take(x.reshape(experts, cap, -1), back, axis=0).reshape(1, experts * cap, -1)

    gate_grad, up_grad = restore(gate_grad), restore(up_grad)
    combine_grad = restore(combine_rel)[:, :, 0]

    head_grads = jnp.concatenate(
        [heads_early] + [a[:, :, width + HD :] for a in late], axis=0
    )
    half_queries[0], gate_grad, up_grad, combine_grad = lax.optimization_barrier(
        (half_queries[0], gate_grad, up_grad, combine_grad)
    )
    query_grad = None
    for half in range(2):
        query_grad = attention(
            half,
            back,
            block_index,
            half_queries[half],
            head_grads,
            all_keys.reshape(-1, QBLK, HD),
            all_values.reshape(-1, QBLK, HD),
            query_grad,
        )
    return (
        query_grad.reshape(experts * toks, HD),
        w_down_grad,
        gate_grad,
        up_grad,
        combine_grad,
    )


def solution(mesh):
    in_specs = (
        P(("mem", "expert"), None),
        P(("mem", "expert"), None),
        P("mem", "expert"),
        P("mem", "expert"),
        P("mem", None),
        P(("mem", "expert"), None),
        P(("mem", "expert"), None),
        P("expert", "mem", None),
        P("expert", "mem", None),
        P("expert", "mem", None),
    )
    out_specs = (
        P("mem", "expert"),
        P("expert", "mem", None),
        P("expert", "mem", None),
        P("expert", "mem", None),
        P("expert", "mem"),
    )
    return jax.shard_map(
        per_device, mesh=mesh, in_specs=in_specs, out_specs=out_specs, check_vma=False
    )
```

```python
import functools

import jax
import jax.numpy as jnp
from jax import lax
from jax.experimental import pallas as pl
from jax.experimental.pallas import tpu as pltpu
from jax.sharding import PartitionSpec as P

HD = 128
QBLK = 128
YS = 4
NEAR = (0, -1, 1)
MID = (-2, 2)
FAR = (-3, 3)
OPPOSITE = (4,)
BANDS = 11


def move(x, zs, dz, dy):
    pairs = [
        (z * YS + y, ((z + dz) % zs) * YS + (y + dy) % YS) for z in range(zs) for y in range(YS)
    ]
    return lax.ppermute(x, "expert", pairs)


def move_opposite(x, zs, mems):
    experts = zs * YS
    pairs = []
    for m in range(mems):
        dz = 2 if m % 2 == 0 else -2
        for z in range(zs):
            for y in range(YS):
                pairs.append((m * experts + z * YS + y, m * experts + ((z + dz) % zs) * YS + y))
    return lax.ppermute(x, ("mem", "expert"), pairs)


def in_bands(block, cap):
    rows = block.astype(jnp.float32)
    fill = BANDS * cap - rows.shape[0]
    rows = jnp.concatenate([rows, jnp.zeros((fill, HD), jnp.float32)], axis=0)
    return [rows[t * cap : (t + 1) * cap].astype(jnp.bfloat16) for t in range(BANDS)]


def placing(ref, width, cap, plane, my_y, keep=None):
    table = ref[:, width:].astype(jnp.float32)
    toks = table.shape[0]
    r0, r1, c0, c1 = (table[:, i : i + 1] for i in range(4))
    lane = lax.broadcasted_iota(jnp.int32, (toks, HD), 1)
    step = sum((lane >= cap * i).astype(jnp.int32) for i in range(1, YS))
    rank = (lane - cap * step).astype(jnp.float32)
    turned = my_y + step
    turned = jnp.where(turned >= YS, turned - YS, turned)
    expert = jnp.where(lane < YS * cap, plane * YS + turned, -1).astype(jnp.float32)
    hit0, hit1 = r0 == expert, r1 == expert
    hit = jnp.where(hit0 | hit1, 1.0, 0.0)
    earlier = lax.broadcasted_iota(jnp.int32, (toks, toks), 1) < lax.broadcasted_iota(
        jnp.int32, (toks, toks), 0
    )
    before = jnp.dot(
        jnp.where(earlier, 1.0, 0.0).astype(jnp.bfloat16),
        hit.astype(jnp.bfloat16),
        preferred_element_type=jnp.float32,
    )
    placed = jnp.where(before == rank, hit, 0.0)
    if keep is not None:
        placed = jnp.where(keep, placed, 0.0)
    value = placed * (jnp.where(hit0, c0, 0.0) + jnp.where(hit1, c1, 0.0))
    weight = jnp.dot(
        value.T.astype(jnp.bfloat16),
        jnp.ones((toks, HD), jnp.bfloat16),
        preferred_element_type=jnp.float32,
    )
    return placed.T.astype(jnp.bfloat16), weight


def head_columns(ref, plane, my_y, j, cap):
    turned = lax.rem(my_y + j, YS)
    first = pl.multiple_of((plane * YS + turned) * HD, HD)
    return in_bands(ref[:, pl.ds(first, HD)], cap)


def dispatch_kernel(n_src, cap, width, info_ref, *refs):
    my_y, plane = info_ref[0], info_ref[1]
    outs = refs[n_src:]
    step = 1024
    for s in range(n_src):
        rows = refs[s]
        onehot, weight = placing(rows, width, cap, plane, my_y)
        for c in range(0, width, step):
            picked = jnp.dot(onehot, rows[:, c : c + step], preferred_element_type=jnp.float32)
            for j in range(YS):
                outs[j][s, :, c : c + step] = picked[j * cap : (j + 1) * cap].astype(jnp.bfloat16)
        for j in range(YS):
            outs[j][s, :, width : width + HD] = weight[j * cap : (j + 1) * cap].astype(
                jnp.bfloat16
            )
            for t, band in enumerate(head_columns(rows, plane, my_y, j, cap)):
                at = width + (1 + t) * HD
                outs[j][s, :, at : at + HD] = band


def dispatch(sources, info, cap):
    n_src = len(sources)
    toks, wide = sources[0].shape
    width = wide - HD
    out_shape = [jax.ShapeDtypeStruct((n_src, cap, wide + BANDS * HD), jnp.bfloat16)] * YS
    whole = pl.BlockSpec(memory_space=pltpu.VMEM)
    return pl.pallas_call(
        functools.partial(dispatch_kernel, n_src, cap, width),
        in_specs=[pl.BlockSpec(memory_space=pltpu.SMEM)] + [whole] * n_src,
        out_specs=[whole] * YS,
        out_shape=out_shape,
        compiler_params=pltpu.CompilerParams(vmem_limit_bytes=28 << 20),
        cost_estimate=pl.CostEstimate(
            flops=2 * n_src * 4 * cap * toks * width,
            bytes_accessed=2 * n_src * width * (toks + 4 * cap),
            transcendentals=0,
        ),
        name="dispatch",
    )(info, *sources)


def pack_kernel(cap, width, info_ref, low_ref, high_ref, *outs):
    my_y, core = info_ref[0], info_ref[1]
    above, below, far_up, far_down = (info_ref[2 + i] for i in range(4))
    step = 1024
    oh_above, w_above = placing(low_ref, width, cap, above, my_y)
    oh_below, w_below = placing(high_ref, width, cap, below, my_y)
    oh_up, w_up = placing(low_ref, width, cap, far_up, my_y, core == 0)
    oh_down, w_down = placing(high_ref, width, cap, far_down, my_y, core != 0)
    for c in range(0, width, step):
        low, high = low_ref[:, c : c + step], high_ref[:, c : c + step]
        picks = (
            jnp.dot(oh_above, low, preferred_element_type=jnp.float32),
            jnp.dot(oh_below, high, preferred_element_type=jnp.float32),
            jnp.dot(oh_up, low, preferred_element_type=jnp.float32)
            + jnp.dot(oh_down, high, preferred_element_type=jnp.float32),
        )
        for out, picked in zip(outs, picks):
            for j in range(YS):
                out[j, :, c : c + step] = picked[j * cap : (j + 1) * cap].astype(jnp.bfloat16)
    for out, w in zip(outs, (w_above, w_below, w_up + w_down)):
        for j in range(YS):
            out[j, :, width : width + HD] = w[j * cap : (j + 1) * cap].astype(jnp.bfloat16)

    def columns(out, ref, plane):
        for j in range(YS):
            for t, band in enumerate(head_columns(ref, plane, my_y, j, cap)):
                at = width + (1 + t) * HD
                out[j, :, at : at + HD] = band

    columns(outs[0], low_ref, above)
    columns(outs[1], high_ref, below)

    @pl.when(core == 0)
    def _():
        columns(outs[2], low_ref, far_up)

    @pl.when(core != 0)
    def _():
        columns(outs[2], high_ref, far_down)


def make_packs(low, high, info, cap):
    toks, wide = low.shape
    width = wide - HD
    whole = pl.BlockSpec(memory_space=pltpu.VMEM)
    return pl.pallas_call(
        functools.partial(pack_kernel, cap, width),
        in_specs=[pl.BlockSpec(memory_space=pltpu.SMEM)] + [whole] * 2,
        out_specs=[whole] * 3,
        out_shape=[jax.ShapeDtypeStruct((YS, cap, wide + BANDS * HD), jnp.bfloat16)] * 3,
        compiler_params=pltpu.CompilerParams(vmem_limit_bytes=28 << 20),
        cost_estimate=pl.CostEstimate(
            flops=2 * 4 * 4 * cap * toks * width,
            bytes_accessed=2 * 2 * width * (toks + 6 * cap),
            transcendentals=0,
        ),
        name="packs",
    )(info, low, high)


def restack_kernel(*refs):
    n = len(refs) - YS
    for j in range(YS):
        for p in range(n):
            refs[n + j][p] = refs[p][j]


def restack(packs):
    whole = pl.BlockSpec(memory_space=pltpu.VMEM)
    shape = (len(packs),) + packs[0].shape[1:]
    size = 2 * 2 * YS * shape[0] * shape[1] * shape[2]
    return pl.pallas_call(
        restack_kernel,
        in_specs=[whole] * len(packs),
        out_specs=[whole] * YS,
        out_shape=[jax.ShapeDtypeStruct(shape, packs[0].dtype)] * YS,
        compiler_params=pltpu.CompilerParams(vmem_limit_bytes=28 << 20),
        cost_estimate=pl.CostEstimate(flops=0, bytes_accessed=size, transcendentals=0),
        name="restack",
    )(*packs)


def unpack_kernel(n_pieces, n_before, width, *refs):
    pieces = refs[:n_pieces]
    rows_out, weight_out, heads_out = refs[-3:]
    at = 0
    if n_before:
        heads_out[:n_before] = refs[n_pieces][...]
    for piece in pieces:
        n = piece.shape[0]
        rows_out[at : at + n] = piece[:, :, :width]
        weight_out[at : at + n] = piece[:, :, width : width + HD]
        heads_out[n_before + at : n_before + at + n] = piece[:, :, width + HD :]
        at += n


def unpack(pieces, heads_before, width):
    n = sum(p.shape[0] for p in pieces)
    cap, wide = pieces[0].shape[1:]
    n_before = 0 if heads_before is None else heads_before.shape[0]
    args = list(pieces) + ([] if heads_before is None else [heads_before])
    whole = pl.BlockSpec(memory_space=pltpu.VMEM)
    return pl.pallas_call(
        functools.partial(unpack_kernel, len(pieces), n_before, width),
        in_specs=[whole] * len(args),
        out_specs=[whole] * 3,
        out_shape=[
            jax.ShapeDtypeStruct((n, cap, width), jnp.bfloat16),
            jax.ShapeDtypeStruct((n, cap, HD), jnp.bfloat16),
            jax.ShapeDtypeStruct((n_before + n, cap, wide - width - HD), jnp.bfloat16),
        ],
        compiler_params=pltpu.CompilerParams(vmem_limit_bytes=32 << 20),
        cost_estimate=pl.CostEstimate(
            flops=0, bytes_accessed=4 * n * cap * wide, transcendentals=0
        ),
        name="unpack",
    )(*args)


def attention_kernel(group, half, back_ref, chosen_ref, q_ref, *refs):
    g_refs = refs[:group]
    k_ref, v_ref = refs[group : group + 2]
    out_ref = refs[-1]
    scale = 1.0 / HD**0.5
    log2e = 1.4426950408889634
    contract_last = (((1,), (1,)), ((), ()))
    cap = g_refs[0].shape[1]
    first = half * QBLK // cap
    skip = half * QBLK - first * cap

    def start(i):
        block = (pl.program_id(0) * group + i) * 2 + half
        ids = [chosen_ref[block, c] for c in range(chosen_ref.shape[1])]
        keys = jnp.concatenate([k_ref[b] for b in ids], axis=0)
        values = jnp.concatenate([v_ref[b] for b in ids], axis=0)
        bands = [
            g_refs[i][0, :, t * HD : (t + 1) * HD].astype(jnp.float32)
            for t in range(first, first - (-(skip + QBLK) // cap))
        ]
        grads = jnp.concatenate(bands, axis=0)[skip : skip + QBLK].astype(jnp.bfloat16)
        scores = lax.dot_general(
            q_ref[i], keys, contract_last, preferred_element_type=jnp.float32
        )
        grad_probs = lax.dot_general(
            grads, values, contract_last, preferred_element_type=jnp.float32
        )
        return keys, scores, grad_probs

    def middle(keys, scores, grad_probs):
        highest = jnp.max(scores, axis=-1, keepdims=True)
        weights = jnp.exp2((scores - highest) * (scale * log2e))
        inverse = 1.0 / jnp.sum(weights, axis=-1, keepdims=True)
        delta = jnp.sum(weights * grad_probs, axis=-1, keepdims=True) * inverse
        return keys, (weights * (grad_probs - delta)).astype(jnp.bfloat16), inverse * scale

    def finish(i, keys, grad_scores, factor):
        total = jnp.dot(grad_scores, keys, preferred_element_type=jnp.float32)
        out_ref[i, 0] = (total * factor).astype(jnp.bfloat16)

    started, halfway = start(0), None
    for i in range(group):
        later = start(i + 1) if i + 1 < group else None
        now = middle(*started)
        if halfway is not None:
            finish(i - 1, *halfway)
        started, halfway = later, now
    finish(group - 1, *halfway)


def attention(half, back, chosen, q, g, keys, values, earlier):
    n_src = back.shape[0]
    group = 4
    full = lambda k, p, c: (0, 0, 0)
    in_specs = [pl.BlockSpec((group, QBLK, HD), lambda k, p, c: (k, 0, 0))]
    for i in range(group):
        in_specs.append(
            pl.BlockSpec((1,) + g.shape[1:], lambda k, p, c, i=i: (p[k * group + i], 0, 0))
        )
    in_specs += [pl.BlockSpec(keys.shape, full), pl.BlockSpec(values.shape, full)]
    args = [q] + [g] * group + [keys, values]
    aliases = {}
    if earlier is not None:
        in_specs.append(pl.BlockSpec(memory_space=pl.ANY))
        args.append(earlier)
        aliases = {2 + len(args) - 1: 0}
    return pl.pallas_call(
        functools.partial(attention_kernel, group, half),
        grid_spec=pltpu.PrefetchScalarGridSpec(
            num_scalar_prefetch=2,
            grid=(n_src // group,),
            in_specs=in_specs,
            out_specs=pl.BlockSpec((group, 1, QBLK, HD), lambda k, p, c: (k, half, 0, 0)),
        ),
        out_shape=jax.ShapeDtypeStruct((n_src, 2, QBLK, HD), jnp.bfloat16),
        input_output_aliases=aliases,
        compiler_params=pltpu.CompilerParams(vmem_limit_bytes=60 << 20),
        cost_estimate=pl.CostEstimate(
            flops=6 * n_src * QBLK * 512 * HD,
            bytes_accessed=6 * n_src * QBLK * HD + 4 * 64 * QBLK * HD,
            transcendentals=n_src * QBLK * 512,
        ),
        name="attention",
    )(back, chosen, *args)


def per_device(
    queries, out_grad, mem_keys, mem_values, block_index, routes, combine, gate_pre, up_pre, w_down
):
    experts = lax.axis_size("expert")
    mems = lax.axis_size("mem")
    zs = experts // YS
    me = lax.axis_index("expert")
    core = lax.axis_index("mem") % 2
    my_z, my_y = me // YS, me % YS
    toks, width = out_grad.shape
    cap = gate_pre.shape[1] // experts
    ff = gate_pre.shape[2]

    own = jnp.concatenate(
        [
            out_grad,
            routes.astype(jnp.bfloat16),
            combine,
            jnp.zeros((toks, HD - routes.shape[1] - combine.shape[1]), jnp.bfloat16),
        ],
        axis=1,
    )
    src = {0: own}
    src[-1] = move(own, zs, 1, 0)
    src[1] = move(own, zs, -1, 0)

    all_keys = lax.all_gather(mem_keys, "mem", axis=0, tiled=True)
    all_values = lax.all_gather(mem_values, "mem", axis=0, tiled=True)
    w_full = lax.all_gather(w_down, "mem", axis=1, tiled=True)[0]

    place = jnp.stack(
        [
            ((my_z + dz) % zs) * YS + (my_y - j) % YS
            for stage in (NEAR, MID, FAR, OPPOSITE)
            for j in range(YS)
            for dz in stage
        ]
    ).astype(jnp.int32)
    back = jnp.zeros((experts,), jnp.int32).at[place].set(jnp.arange(experts, dtype=jnp.int32))

    gate_rel = jnp.take(gate_pre.reshape(experts, cap, ff), place, axis=0).reshape(-1, ff)
    up_rel = jnp.take(up_pre.reshape(experts, cap, ff), place, axis=0).reshape(-1, ff)
    gate_val = gate_rel.astype(jnp.float32)
    up_val = up_rel.astype(jnp.float32)
    sigmoid_gate = jax.nn.sigmoid(gate_val)
    silu_gate = gate_val * sigmoid_gate
    hidden = silu_gate * up_val

    src[-2] = move(src[-1], zs, 1, 0)
    src[2] = move(src[1], zs, -1, 0)
    here = jnp.stack([my_y, my_z]).astype(jnp.int32)

    def spread(x):
        return [x[0]] + [move(x[j], zs, 0, j) for j in range(1, YS)]

    near = spread(dispatch([src[dz] for dz in NEAR], here, cap))
    targets = [my_y, core] + [(my_z + dz) % zs for dz in (1, -1, 2, -2)]
    packs = make_packs(src[-2], src[2], jnp.stack(targets).astype(jnp.int32), cap)
    far = [move(packs[0], zs, 1, 0), move(packs[1], zs, -1, 0), move_opposite(packs[2], zs, mems)]
    low, high, packs, near = lax.optimization_barrier((src[-2], src[2], packs, near))
    mid = spread(dispatch([low, high], here, cap))

    by_half = [
        jnp.swapaxes(queries[h * QBLK : (h + 1) * QBLK].reshape(QBLK, experts, HD), 0, 1)
        for h in range(2)
    ]
    opposite = far.pop()
    far = restack(far)
    early = near + mid
    early, _ = lax.optimization_barrier((early, far))
    by_half, _, _ = lax.optimization_barrier((by_half, far, opposite))
    half_queries = [
        lax.all_to_all(by_half[0], "expert", split_axis=0, concat_axis=0, tiled=True)
    ]
    late = spread(far) + spread([opposite[j : j + 1] for j in range(YS)])
    n_early = YS * (len(NEAR) + len(MID)) * cap

    def slot_down(rows, weights, span):
        weight_col = weights.reshape(-1, HD)[:, :1].astype(jnp.float32)
        weighted = (weight_col * hidden[span]).astype(jnp.bfloat16)
        down = lax.dot_general(
            weighted, rows, (((0,), (0,)), ((), ())), preferred_element_type=jnp.float32
        )
        return down, weight_col

    def slot_grads(rows, weight_col, span):
        back_grad = lax.dot_general(
            rows, w_full, (((1,), (1,)), ((), ())), preferred_element_type=jnp.float32
        )
        gate, up, sig = gate_val[span], up_val[span], sigmoid_gate[span]
        hidden_grad = weight_col * back_grad
        return (
            (hidden_grad * up * sig * (1.0 + gate * (1.0 - sig))).astype(jnp.bfloat16),
            (hidden_grad * silu_gate[span]).astype(jnp.bfloat16),
            jnp.sum(hidden[span] * back_grad, axis=-1),
        )

    span = slice(0, n_early)
    rows, weights, heads_early = unpack(early, None, width)
    rows = rows.reshape(-1, width)
    down_early, weight_col = slot_down(rows, weights, span)
    down_early = down_early.astype(jnp.bfloat16)
    grads_early = slot_grads(rows, weight_col, span)
    half_queries[0], late, by_half[1], down_early, grads_early, heads_early = (
        lax.optimization_barrier(
            (half_queries[0], late, by_half[1], down_early, grads_early, heads_early)
        )
    )
    half_queries.append(
        lax.all_to_all(by_half[1], "expert", split_axis=0, concat_axis=0, tiled=True)
    )
    span = slice(n_early, None)
    rows, weights, head_grads = unpack(late, heads_early, width)
    rows = rows.reshape(-1, width)
    down_late, weight_col = slot_down(rows, weights, span)
    down_total = (down_early.astype(jnp.float32) + down_late).astype(jnp.bfloat16)
    w_down_grad = lax.psum_scatter(down_total, "mem", scatter_dimension=0, tiled=True)[None]
    rows, _ = lax.optimization_barrier((rows, down_total))
    grads_late = slot_grads(rows, weight_col, span)
    gate_grad, up_grad, combine_rel = (
        jnp.concatenate(r, axis=0) for r in zip(grads_early, grads_late)
    )

    def restore(x):
        return jnp.take(x.reshape(experts, cap, -1), back, axis=0).reshape(1, experts * cap, -1)

    gate_grad, up_grad = restore(gate_grad), restore(up_grad)
    combine_grad = restore(combine_rel)[:, :, 0]

    half_queries[0], gate_grad, up_grad, combine_grad = lax.optimization_barrier(
        (half_queries[0], gate_grad, up_grad, combine_grad)
    )
    query_grad = None
    for half in range(2):
        query_grad = attention(
            half,
            back,
            block_index,
            half_queries[half],
            head_grads,
            all_keys.reshape(-1, QBLK, HD),
            all_values.reshape(-1, QBLK, HD),
            query_grad,
        )
    return (
        query_grad.reshape(experts * toks, HD),
        w_down_grad,
        gate_grad,
        up_grad,
        combine_grad,
    )


def solution(mesh):
    in_specs = (
        P(("mem", "expert"), None),
        P(("mem", "expert"), None),
        P("mem", "expert"),
        P("mem", "expert"),
        P("mem", None),
        P(("mem", "expert"), None),
        P(("mem", "expert"), None),
        P("expert", "mem", None),
        P("expert", "mem", None),
        P("expert", "mem", None),
    )
    out_specs = (
        P("mem", "expert"),
        P("expert", "mem", None),
        P("expert", "mem", None),
        P("expert", "mem", None),
        P("expert", "mem"),
    )
    return jax.shard_map(
        per_device, mesh=mesh, in_specs=in_specs, out_specs=out_specs, check_vma=False
    )
```

```python
import functools

import jax
import jax.numpy as jnp
from jax import lax
from jax.experimental import pallas as pl
from jax.experimental.pallas import tpu as pltpu
from jax.sharding import PartitionSpec as P

HD = 128
QBLK = 128
YS = 4
NEAR = (0, -1, 1)
MID = (-2, 2)
FAR = (-3, 3)
OPPOSITE = (4,)
BANDS = 11


def move(x, zs, dz, dy):
    pairs = [
        (z * YS + y, ((z + dz) % zs) * YS + (y + dy) % YS) for z in range(zs) for y in range(YS)
    ]
    return lax.ppermute(x, "expert", pairs)


def move_opposite(x, zs, mems):
    experts = zs * YS
    pairs = []
    for m in range(mems):
        dz = 2 if m % 2 == 0 else -2
        for z in range(zs):
            for y in range(YS):
                pairs.append((m * experts + z * YS + y, m * experts + ((z + dz) % zs) * YS + y))
    return lax.ppermute(x, ("mem", "expert"), pairs)


def whole(x):
    return pl.BlockSpec(x.shape, lambda i: (0,) * len(x.shape))


def in_bands(block, cap):
    rows = block.astype(jnp.float32)
    fill = BANDS * cap - rows.shape[0]
    rows = jnp.concatenate([rows, jnp.zeros((fill, HD), jnp.float32)], axis=0)
    return [rows[t * cap : (t + 1) * cap].astype(jnp.bfloat16) for t in range(BANDS)]


def placing(ref, width, cap, plane, my_y, keep=None):
    table = ref[:, width:].astype(jnp.float32)
    toks = table.shape[0]
    r0, r1, c0, c1 = (table[:, i : i + 1] for i in range(4))
    lane = lax.broadcasted_iota(jnp.int32, (toks, HD), 1)
    step = sum((lane >= cap * i).astype(jnp.int32) for i in range(1, YS))
    rank = (lane - cap * step).astype(jnp.float32)
    turned = my_y + step
    turned = jnp.where(turned >= YS, turned - YS, turned)
    expert = jnp.where(lane < YS * cap, plane * YS + turned, -1).astype(jnp.float32)
    hit0, hit1 = r0 == expert, r1 == expert
    hit = jnp.where(hit0 | hit1, 1.0, 0.0)
    earlier = lax.broadcasted_iota(jnp.int32, (toks, toks), 1) < lax.broadcasted_iota(
        jnp.int32, (toks, toks), 0
    )
    before = jnp.dot(
        jnp.where(earlier, 1.0, 0.0).astype(jnp.bfloat16),
        hit.astype(jnp.bfloat16),
        preferred_element_type=jnp.float32,
    )
    placed = jnp.where(before == rank, hit, 0.0)
    if keep is not None:
        placed = jnp.where(keep, placed, 0.0)
    value = placed * (jnp.where(hit0, c0, 0.0) + jnp.where(hit1, c1, 0.0))
    weight = jnp.dot(
        value.T.astype(jnp.bfloat16),
        jnp.ones((toks, HD), jnp.bfloat16),
        preferred_element_type=jnp.float32,
    )
    return placed.T.astype(jnp.bfloat16), weight


def head_columns(ref, plane, my_y, j, cap):
    turned = lax.rem(my_y + j, YS)
    first = pl.multiple_of((plane * YS + turned) * HD, HD)
    return in_bands(ref[:, pl.ds(first, HD)], cap)


def dispatch_kernel(n_src, cap, width, info_ref, *refs):
    my_y, plane = info_ref[0], info_ref[1]
    outs = refs[n_src:]
    step = 1024
    for s in range(n_src):
        rows = refs[s]
        onehot, weight = placing(rows, width, cap, plane, my_y)
        for c in range(0, width, step):
            picked = jnp.dot(onehot, rows[:, c : c + step], preferred_element_type=jnp.float32)
            for j in range(YS):
                outs[j][s, :, c : c + step] = picked[j * cap : (j + 1) * cap].astype(jnp.bfloat16)
        for j in range(YS):
            outs[j][s, :, width : width + HD] = weight[j * cap : (j + 1) * cap].astype(
                jnp.bfloat16
            )
            for t, band in enumerate(head_columns(rows, plane, my_y, j, cap)):
                at = width + (1 + t) * HD
                outs[j][s, :, at : at + HD] = band


def dispatch(sources, info, cap):
    n_src = len(sources)
    toks, wide = sources[0].shape
    width = wide - HD
    out_shape = [jax.ShapeDtypeStruct((n_src, cap, wide + BANDS * HD), jnp.bfloat16)] * YS
    return pl.pallas_call(
        functools.partial(dispatch_kernel, n_src, cap, width),
        grid=(1,),
        in_specs=[pl.BlockSpec(memory_space=pltpu.SMEM)] + [whole(x) for x in sources],
        out_specs=[whole(x) for x in out_shape],
        out_shape=out_shape,
        compiler_params=pltpu.CompilerParams(vmem_limit_bytes=58 << 20),
        cost_estimate=pl.CostEstimate(
            flops=2 * n_src * 4 * cap * toks * width,
            bytes_accessed=2 * n_src * width * (toks + 4 * cap),
            transcendentals=0,
        ),
        name="dispatch",
    )(info, *sources)


def pack_kernel(cap, width, info_ref, low_ref, high_ref, *outs):
    my_y, core = info_ref[0], info_ref[1]
    above, below, far_up, far_down = (info_ref[2 + i] for i in range(4))
    step = 1024
    oh_above, w_above = placing(low_ref, width, cap, above, my_y)
    oh_below, w_below = placing(high_ref, width, cap, below, my_y)
    oh_up, w_up = placing(low_ref, width, cap, far_up, my_y, core == 0)
    oh_down, w_down = placing(high_ref, width, cap, far_down, my_y, core != 0)
    for c in range(0, width, step):
        low, high = low_ref[:, c : c + step], high_ref[:, c : c + step]
        picks = (
            jnp.dot(oh_above, low, preferred_element_type=jnp.float32),
            jnp.dot(oh_below, high, preferred_element_type=jnp.float32),
            jnp.dot(oh_up, low, preferred_element_type=jnp.float32)
            + jnp.dot(oh_down, high, preferred_element_type=jnp.float32),
        )
        for out, picked in zip(outs, picks):
            for j in range(YS):
                out[j, :, c : c + step] = picked[j * cap : (j + 1) * cap].astype(jnp.bfloat16)
    for out, w in zip(outs, (w_above, w_below, w_up + w_down)):
        for j in range(YS):
            out[j, :, width : width + HD] = w[j * cap : (j + 1) * cap].astype(jnp.bfloat16)

    def columns(out, ref, plane):
        for j in range(YS):
            for t, band in enumerate(head_columns(ref, plane, my_y, j, cap)):
                at = width + (1 + t) * HD
                out[j, :, at : at + HD] = band

    columns(outs[0], low_ref, above)
    columns(outs[1], high_ref, below)

    @pl.when(core == 0)
    def _():
        columns(outs[2], low_ref, far_up)

    @pl.when(core != 0)
    def _():
        columns(outs[2], high_ref, far_down)


def make_packs(low, high, info, cap):
    toks, wide = low.shape
    width = wide - HD
    out_shape = [jax.ShapeDtypeStruct((YS, cap, wide + BANDS * HD), jnp.bfloat16)] * 3
    return pl.pallas_call(
        functools.partial(pack_kernel, cap, width),
        grid=(1,),
        in_specs=[pl.BlockSpec(memory_space=pltpu.SMEM), whole(low), whole(high)],
        out_specs=[whole(x) for x in out_shape],
        out_shape=out_shape,
        compiler_params=pltpu.CompilerParams(vmem_limit_bytes=58 << 20),
        cost_estimate=pl.CostEstimate(
            flops=2 * 4 * 4 * cap * toks * width,
            bytes_accessed=2 * 2 * width * (toks + 6 * cap),
            transcendentals=0,
        ),
        name="packs",
    )(info, low, high)


def restack_kernel(*refs):
    n = len(refs) - YS
    for j in range(YS):
        for p in range(n):
            refs[n + j][p] = refs[p][j]


def restack(packs):
    shape = (len(packs),) + packs[0].shape[1:]
    out_shape = [jax.ShapeDtypeStruct(shape, packs[0].dtype)] * YS
    size = 2 * 2 * YS * shape[0] * shape[1] * shape[2]
    return pl.pallas_call(
        restack_kernel,
        grid=(1,),
        in_specs=[whole(x) for x in packs],
        out_specs=[whole(x) for x in out_shape],
        out_shape=out_shape,
        compiler_params=pltpu.CompilerParams(vmem_limit_bytes=58 << 20),
        cost_estimate=pl.CostEstimate(flops=0, bytes_accessed=size, transcendentals=0),
        name="restack",
    )(*packs)


def unpack_kernel(n_pieces, n_before, width, *refs):
    pieces = refs[:n_pieces]
    rows_out, weight_out, heads_out = refs[-3:]
    at = 0
    if n_before:
        heads_out[:n_before] = refs[n_pieces][...]
    for piece in pieces:
        n = piece.shape[0]
        rows_out[at : at + n] = piece[:, :, :width]
        weight_out[at : at + n] = piece[:, :, width : width + HD]
        heads_out[n_before + at : n_before + at + n] = piece[:, :, width + HD :]
        at += n


def unpack(pieces, heads_before, width):
    n = sum(p.shape[0] for p in pieces)
    cap, wide = pieces[0].shape[1:]
    n_before = 0 if heads_before is None else heads_before.shape[0]
    args = list(pieces) + ([] if heads_before is None else [heads_before])
    out_shape = [
        jax.ShapeDtypeStruct((n, cap, width), jnp.bfloat16),
        jax.ShapeDtypeStruct((n, cap, HD), jnp.bfloat16),
        jax.ShapeDtypeStruct((n_before + n, cap, wide - width - HD), jnp.bfloat16),
    ]
    return pl.pallas_call(
        functools.partial(unpack_kernel, len(pieces), n_before, width),
        grid=(1,),
        in_specs=[whole(x) for x in args],
        out_specs=[whole(x) for x in out_shape],
        out_shape=out_shape,
        compiler_params=pltpu.CompilerParams(vmem_limit_bytes=58 << 20),
        cost_estimate=pl.CostEstimate(
            flops=0, bytes_accessed=4 * n * cap * wide, transcendentals=0
        ),
        name="unpack",
    )(*args)


def add_down_kernel(weight_ref, hidden_ref, rows_ref, early_ref, out_ref, weighted):
    @pl.when(pl.program_id(0) == 0)
    def _():
        weighted[...] = (hidden_ref[...] * weight_ref[...]).astype(jnp.bfloat16)

    late = jnp.dot(weighted[...], rows_ref[...], preferred_element_type=jnp.float32)
    out_ref[...] = (early_ref[...].astype(jnp.float32) + late).astype(jnp.bfloat16)


def add_down(weight_row, hidden_t, rows, early):
    n, width = rows.shape
    ff = hidden_t.shape[0]
    step = 512
    return pl.pallas_call(
        add_down_kernel,
        grid=(width // step,),
        in_specs=[
            pl.BlockSpec((1, n), lambda c: (0, 0)),
            pl.BlockSpec((ff, n), lambda c: (0, 0)),
            pl.BlockSpec((n, step), lambda c: (0, c)),
            pl.BlockSpec((ff, step), lambda c: (0, c)),
        ],
        out_specs=pl.BlockSpec((ff, step), lambda c: (0, c)),
        out_shape=jax.ShapeDtypeStruct((ff, width), jnp.bfloat16),
        scratch_shapes=[pltpu.VMEM((ff, n), jnp.bfloat16)],
        compiler_params=pltpu.CompilerParams(vmem_limit_bytes=58 << 20),
        cost_estimate=pl.CostEstimate(
            flops=2 * ff * n * width, bytes_accessed=2 * width * (n + 2 * ff), transcendentals=0
        ),
        name="add_down",
    )(weight_row, hidden_t, rows, early)


def attention_kernel(group, half, back_ref, chosen_ref, q_ref, *refs):
    g_refs = refs[:group]
    k_ref, v_ref = refs[group : group + 2]
    out_ref = refs[-1]
    scale = 1.0 / HD**0.5
    log2e = 1.4426950408889634
    contract_last = (((1,), (1,)), ((), ()))
    cap = g_refs[0].shape[1]
    first = half * QBLK // cap
    skip = half * QBLK - first * cap

    def start(i):
        block = (pl.program_id(0) * group + i) * 2 + half
        ids = [chosen_ref[block, c] for c in range(chosen_ref.shape[1])]
        keys = jnp.concatenate([k_ref[b] for b in ids], axis=0)
        values = jnp.concatenate([v_ref[b] for b in ids], axis=0)
        bands = [
            g_refs[i][0, :, t * HD : (t + 1) * HD].astype(jnp.float32)
            for t in range(first, first - (-(skip + QBLK) // cap))
        ]
        grads = jnp.concatenate(bands, axis=0)[skip : skip + QBLK].astype(jnp.bfloat16)
        scores = lax.dot_general(
            q_ref[i], keys, contract_last, preferred_element_type=jnp.float32
        )
        grad_probs = lax.dot_general(
            grads, values, contract_last, preferred_element_type=jnp.float32
        )
        return keys, scores, grad_probs

    def middle(keys, scores, grad_probs):
        highest = jnp.max(scores, axis=-1, keepdims=True)
        weights = jnp.exp2((scores - highest) * (scale * log2e))
        inverse = 1.0 / jnp.sum(weights, axis=-1, keepdims=True)
        delta = jnp.sum(weights * grad_probs, axis=-1, keepdims=True) * inverse
        return keys, (weights * (grad_probs - delta)).astype(jnp.bfloat16), inverse * scale

    def finish(i, keys, grad_scores, factor):
        total = jnp.dot(grad_scores, keys, preferred_element_type=jnp.float32)
        out_ref[i, 0] = (total * factor).astype(jnp.bfloat16)

    started, halfway = start(0), None
    for i in range(group):
        later = start(i + 1) if i + 1 < group else None
        now = middle(*started)
        if halfway is not None:
            finish(i - 1, *halfway)
        started, halfway = later, now
    finish(group - 1, *halfway)


def attention(half, back, chosen, q, g, keys, values, earlier):
    n_src = back.shape[0]
    group = 4
    full = lambda k, p, c: (0, 0, 0)
    in_specs = [pl.BlockSpec((group, QBLK, HD), lambda k, p, c: (k, 0, 0))]
    for i in range(group):
        in_specs.append(
            pl.BlockSpec((1,) + g.shape[1:], lambda k, p, c, i=i: (p[k * group + i], 0, 0))
        )
    in_specs += [pl.BlockSpec(keys.shape, full), pl.BlockSpec(values.shape, full)]
    args = [q] + [g] * group + [keys, values]
    aliases = {}
    if earlier is not None:
        in_specs.append(pl.BlockSpec(memory_space=pl.ANY))
        args.append(earlier)
        aliases = {2 + len(args) - 1: 0}
    return pl.pallas_call(
        functools.partial(attention_kernel, group, half),
        grid_spec=pltpu.PrefetchScalarGridSpec(
            num_scalar_prefetch=2,
            grid=(n_src // group,),
            in_specs=in_specs,
            out_specs=pl.BlockSpec((group, 1, QBLK, HD), lambda k, p, c: (k, half, 0, 0)),
        ),
        out_shape=jax.ShapeDtypeStruct((n_src, 2, QBLK, HD), jnp.bfloat16),
        input_output_aliases=aliases,
        compiler_params=pltpu.CompilerParams(vmem_limit_bytes=60 << 20),
        cost_estimate=pl.CostEstimate(
            flops=6 * n_src * QBLK * 512 * HD,
            bytes_accessed=6 * n_src * QBLK * HD + 4 * 64 * QBLK * HD,
            transcendentals=n_src * QBLK * 512,
        ),
        name="attention",
    )(back, chosen, *args)


def per_device(
    queries, out_grad, mem_keys, mem_values, block_index, routes, combine, gate_pre, up_pre, w_down
):
    experts = lax.axis_size("expert")
    mems = lax.axis_size("mem")
    zs = experts // YS
    me = lax.axis_index("expert")
    core = lax.axis_index("mem") % 2
    my_z, my_y = me // YS, me % YS
    toks, width = out_grad.shape
    cap = gate_pre.shape[1] // experts
    ff = gate_pre.shape[2]

    own = jnp.concatenate(
        [
            out_grad,
            routes.astype(jnp.bfloat16),
            combine,
            jnp.zeros((toks, HD - routes.shape[1] - combine.shape[1]), jnp.bfloat16),
        ],
        axis=1,
    )
    src = {0: own}
    src[-1] = move(own, zs, 1, 0)
    src[1] = move(own, zs, -1, 0)

    all_keys = lax.all_gather(mem_keys, "mem", axis=0, tiled=True)
    all_values = lax.all_gather(mem_values, "mem", axis=0, tiled=True)
    w_full = lax.all_gather(w_down, "mem", axis=1, tiled=True)[0]

    place = jnp.stack(
        [
            ((my_z + dz) % zs) * YS + (my_y - j) % YS
            for stage in (NEAR, MID, FAR, OPPOSITE)
            for j in range(YS)
            for dz in stage
        ]
    ).astype(jnp.int32)
    back = jnp.zeros((experts,), jnp.int32).at[place].set(jnp.arange(experts, dtype=jnp.int32))

    gate_rel = jnp.take(gate_pre.reshape(experts, cap, ff), place, axis=0).reshape(-1, ff)
    up_rel = jnp.take(up_pre.reshape(experts, cap, ff), place, axis=0).reshape(-1, ff)
    gate_val = gate_rel.astype(jnp.float32)
    up_val = up_rel.astype(jnp.float32)
    sigmoid_gate = jax.nn.sigmoid(gate_val)
    silu_gate = gate_val * sigmoid_gate
    hidden = silu_gate * up_val

    src[-2] = move(src[-1], zs, 1, 0)
    src[2] = move(src[1], zs, -1, 0)
    here = jnp.stack([my_y, my_z]).astype(jnp.int32)

    def spread(x):
        return [x[0]] + [move(x[j], zs, 0, j) for j in range(1, YS)]

    near = spread(dispatch([src[dz] for dz in NEAR], here, cap))
    targets = [my_y, core] + [(my_z + dz) % zs for dz in (1, -1, 2, -2)]
    packs = make_packs(src[-2], src[2], jnp.stack(targets).astype(jnp.int32), cap)
    far = [move(packs[0], zs, 1, 0), move(packs[1], zs, -1, 0), move_opposite(packs[2], zs, mems)]
    low, high, packs, near = lax.optimization_barrier((src[-2], src[2], packs, near))
    mid = spread(dispatch([low, high], here, cap))

    by_half = [
        jnp.swapaxes(queries[h * QBLK : (h + 1) * QBLK].reshape(QBLK, experts, HD), 0, 1)
        for h in range(2)
    ]
    opposite = far.pop()
    far = restack(far)
    early = near + mid
    early, _ = lax.optimization_barrier((early, far))
    by_half, _, _ = lax.optimization_barrier((by_half, far, opposite))
    half_queries = [
        lax.all_to_all(by_half[0], "expert", split_axis=0, concat_axis=0, tiled=True)
    ]
    late = spread(far) + spread([opposite[j : j + 1] for j in range(YS)])
    n_early = YS * (len(NEAR) + len(MID)) * cap

    def slot_down(rows, weights, span):
        weight_col = weights.reshape(-1, HD)[:, :1].astype(jnp.float32)
        weighted = (weight_col * hidden[span]).astype(jnp.bfloat16)
        down = lax.dot_general(
            weighted, rows, (((0,), (0,)), ((), ())), preferred_element_type=jnp.float32
        )
        return down, weight_col

    def slot_grads(rows, weight_col, span):
        back_grad = lax.dot_general(
            rows, w_full, (((1,), (1,)), ((), ())), preferred_element_type=jnp.float32
        )
        gate, up, sig = gate_val[span], up_val[span], sigmoid_gate[span]
        hidden_grad = weight_col * back_grad
        return (
            (hidden_grad * up * sig * (1.0 + gate * (1.0 - sig))).astype(jnp.bfloat16),
            (hidden_grad * silu_gate[span]).astype(jnp.bfloat16),
            jnp.sum(hidden[span] * back_grad, axis=-1),
        )

    span = slice(0, n_early)
    rows, weights, heads_early = unpack(early, None, width)
    rows = rows.reshape(-1, width)
    down_early, weight_col = slot_down(rows, weights, span)
    down_early = down_early.astype(jnp.bfloat16)
    grads_early = slot_grads(rows, weight_col, span)
    hidden_late = hidden[n_early:].T
    half_queries[0], late, by_half[1], down_early, grads_early, heads_early, hidden_late = (
        lax.optimization_barrier(
            (half_queries[0], late, by_half[1], down_early, grads_early, heads_early, hidden_late)
        )
    )
    half_queries.append(
        lax.all_to_all(by_half[1], "expert", split_axis=0, concat_axis=0, tiled=True)
    )
    span = slice(n_early, None)
    rows, weights, head_grads = unpack(late, heads_early, width)
    rows = rows.reshape(-1, width)
    weight_col = weights.reshape(-1, HD)[:, :1].astype(jnp.float32)
    down_total = add_down(weight_col.reshape(1, -1), hidden_late, rows, down_early)
    w_down_grad = lax.psum_scatter(down_total, "mem", scatter_dimension=0, tiled=True)[None]
    rows, _ = lax.optimization_barrier((rows, down_total))
    grads_late = slot_grads(rows, weight_col, span)
    gate_grad, up_grad, combine_rel = (
        jnp.concatenate(r, axis=0) for r in zip(grads_early, grads_late)
    )

    def restore(x):
        return jnp.take(x.reshape(experts, cap, -1), back, axis=0).reshape(1, experts * cap, -1)

    gate_grad, up_grad = restore(gate_grad), restore(up_grad)
    combine_grad = restore(combine_rel)[:, :, 0]

    half_queries[0], gate_grad, up_grad, combine_grad = lax.optimization_barrier(
        (half_queries[0], gate_grad, up_grad, combine_grad)
    )
    query_grad = None
    for half in range(2):
        query_grad = attention(
            half,
            back,
            block_index,
            half_queries[half],
            head_grads,
            all_keys.reshape(-1, QBLK, HD),
            all_values.reshape(-1, QBLK, HD),
            query_grad,
        )
    return (
        query_grad.reshape(experts * toks, HD),
        w_down_grad,
        gate_grad,
        up_grad,
        combine_grad,
    )


def solution(mesh):
    in_specs = (
        P(("mem", "expert"), None),
        P(("mem", "expert"), None),
        P("mem", "expert"),
        P("mem", "expert"),
        P("mem", None),
        P(("mem", "expert"), None),
        P(("mem", "expert"), None),
        P("expert", "mem", None),
        P("expert", "mem", None),
        P("expert", "mem", None),
    )
    out_specs = (
        P("mem", "expert"),
        P("expert", "mem", None),
        P("expert", "mem", None),
        P("expert", "mem", None),
        P("expert", "mem"),
    )
    return jax.shard_map(
        per_device, mesh=mesh, in_specs=in_specs, out_specs=out_specs, check_vma=False
    )
```
